512 devices in a mesh: dp: 64 (over x, y, core), shard: 8 (over z).
Axes of the slice: x: 4, y: 8, z: 8, core: 2. Of those that a mesh axis runs over, the one named last changes fastest.
Arguments:
- layer_input: bfloat16 [49152, 3968], P('dp', 'shard'), may hold values from -6 to 6
- output_grad: bfloat16 [49152, 1984], P('dp', 'shard'), may hold values from -0.21875 to 0.21875
- error_buffer: bfloat16 [64, 3968, 1984], P('dp', 'shard'), may hold values from -4 to 4
- q_start: float32 [1984, 32], P('shard'), may hold values from -6 to 6
Outputs:
- new_error: bfloat16 [64, 3968, 1984], P('dp', 'shard')
- q_factor: float32 [1984, 32], P('shard')
The draws below stay inside these ranges and needn't reach their ends.
All inputs are finite; a program needn't handle non-finite values.
Results may differ from the reference program's by a relative error of at most 0.0075.
Values may be sent and summed in bfloat16 or wider, within the bound.
A program may use at most 64 MiB of HBM per device.

```python
import jax
import jax.numpy as jnp
from jax import lax

D = 3968
COLS = 1984
RANK = 32
TOK = 768
TOKENS = 49152
N_DP = 64


def levels(rng, shape, shards, low, largest):
    def one(position, shards_of):
        steps = jax.random.uniform(jax.random.fold_in(jax.random.fold_in(rng, 6), position), (shards_of,), jnp.float32, low / len(shards), largest / len(shards))
        return jnp.repeat(jnp.exp(steps), shape[position] // shards_of).reshape((-1,) + (1,) * (len(shape) - position - 1))

    level = one(*shards[0])
    for cut in shards[1:]:
        level = level * one(*cut)
    return level


def centred(stream_key, extent, width, limit, shards=(), held_as=jnp.bfloat16):
    array = jax.random.normal(stream_key, extent, jnp.float32) * width
    if len(shards) > 0:
        array = levels(stream_key, extent, shards, -0.22, 0.18) * array
    return jnp.clip(array, min=-limit, max=limit).astype(held_as)


def setup_inputs(seed: int = 0) -> dict:
    key_of = jax.random.split(jax.random.key(seed), 5)
    layer_input = centred(key_of[0], (TOKENS, D), 1.0, 6.0, ((0, 64), (1, 8)))
    output_grad = centred(key_of[1], (TOKENS, COLS), TOK ** -0.5, 0.21875, ((0, 64), (1, 8)))
    error_buffer = centred(key_of[2], (N_DP, D, COLS), 0.5, 4.0, ((0, 64), (1, 8)))
    q_start = centred(key_of[3], (COLS, RANK), 1.0, 6.0, ((0, 8),), jnp.float32)
    return dict(layer_input=layer_input, output_grad=output_grad, error_buffer=error_buffer, q_start=q_start)


def reference(layer_input, output_grad, error_buffer, q_start):
    inputs = layer_input.reshape(N_DP, TOK, D)
    grads = output_grad.reshape(N_DP, TOK, COLS)

    def one_worker(pieces):
        x_rows, y_rows, err = pieces
        gradient = jnp.dot(x_rows.T.astype(jnp.float32), y_rows.astype(jnp.float32), preferred_element_type=jnp.float32)
        return gradient + err.astype(jnp.float32)
    merged = lax.map(one_worker, (inputs, grads, error_buffer))
    p_sum = jnp.einsum('wdc,cr->dr', merged, q_start, precision=lax.Precision.HIGHEST)
    gram = jnp.dot(p_sum.T, p_sum, precision=lax.Precision.HIGHEST)
    lower = jnp.linalg.cholesky(gram)
    p_hat = jax.scipy.linalg.solve_triangular(lower, p_sum.T, lower=True).T
    q_factor = jnp.einsum('wdc,dr->cr', merged, p_hat, precision=lax.Precision.HIGHEST) / N_DP
    approx = jnp.dot(p_hat, q_factor.T, precision=lax.Precision.HIGHEST)
    new_error = (merged - approx[None]).astype(jnp.bfloat16)
    return (new_error, q_factor)
```

```python
import functools

import jax
import jax.numpy as jnp
from jax import lax
from jax.experimental import pallas as pl
from jax.experimental.pallas import tpu as pltpu
from jax.sharding import PartitionSpec as P

MESH = pl.DeviceIdType.MESH
F32, BF16 = jnp.float32, jnp.bfloat16
NX, NY, NZ = 4, 8, 8
G = 2 * NX
TOK, ROWS, COLS, OWN, RANK = 768, 496, 1984, 248, 32
SUBS = 4
SUB = TOK // SUBS
WINDOW = 3
WORKERS = 64
HIGHEST = lax.Precision.HIGHEST


def halves(a):
    high = a.astype(BF16)
    low = (a - high.astype(F32)).astype(BF16)
    return jnp.concatenate([high, low], axis=0)


def folded(a):
    return a[:RANK] + a[RANK:]


def nn(a, b):
    return lax.dot_general(a, b, (((1,), (0,)), ((), ())), preferred_element_type=F32)


def nt(a, b):
    return lax.dot_general(a, b, (((1,), (1,)), ((), ())), preferred_element_type=F32)


def inverse_factor(gram):
    row = lax.broadcasted_iota(jnp.int32, (RANK, RANK), 0)
    col = lax.broadcasted_iota(jnp.int32, (RANK, RANK), 1)
    left, right = gram, jnp.where(row == col, 1.0, 0.0).astype(F32)
    index = lax.broadcasted_iota(jnp.int32, (RANK, 1), 0)
    for j in range(RANK):
        scale = 1.0 / jnp.sqrt(left[j : j + 1, j : j + 1])
        left_row, right_row = left[j : j + 1, :] * scale, right[j : j + 1, :] * scale
        column = left[:, j : j + 1] * scale
        below = jnp.where(index > j, column, 0.0)
        left = left - below * left_row
        right = jnp.where(row == j, right_row, right - below * right_row)
    return right


def kernel(
    x_hbm, y_hbm, e_hbm, q_hbm, out_hbm, qout,
    xv, xt, yb, ev, qv,
    tp, tr, tf, qst, qz, qall, qfull,
    pp, pr, py, pyr, pa,
    gz, gzr,
    rp, rr, ry, ryr, rz, rzr, rya, ra,
    mrg, outv, qpad, qnat,
    in_sem, out_sem, ring_s, ring_r, small_s, small_r,
):
    dp, z = lax.axis_index("dp"), lax.axis_index("shard")
    x, y, c = dp // (2 * NY), (dp // 2) % NY, dp % 2
    m = 2 * x + c

    def device(x_, y_, c_, z_):
        return ((x_ * NY + y_) * 2 + c_, z_)

    z_peers = [device(x, y, c, (z + i) % NZ) for i in range(1, NZ)]
    y_peers = [device(x, (y + i) % NY, c, z) for i in range(1, NY)]
    g_peers = [device(((m + i) % G) // 2, y, (m + i) % 2, z) for i in range(1, G)]

    loads = [
        pltpu.make_async_copy(src, dst, in_sem.at[i])
        for i, (src, dst) in enumerate([(y_hbm, yb.at[z]), (q_hbm, qv), (x_hbm, xv), (e_hbm, ev)])
    ]
    for load in loads:
        load.start()
    barrier = pltpu.get_barrier_semaphore()
    for peer in z_peers + y_peers + g_peers:
        pl.semaphore_signal(barrier, inc=1, device_id=peer, device_id_type=MESH)

    started = []

    def exchange(stage, peers, src, dst):
        copies = []
        for i, peer in enumerate(peers, 1):
            copy = pltpu.make_async_remote_copy(
                src_ref=src(i), dst_ref=dst(i), send_sem=small_s.at[stage, i - 1], recv_sem=small_r.at[stage, i - 1],
                device_id=peer, device_id_type=MESH,
            )
            copy.start()
            copies.append(copy)
        started.extend(copies)
        return copies

    def arrived(copies):
        for copy in copies:
            copy.wait_recv()

    def in_order(parts, place, count):
        total = parts[place]
        for owner in range(1, count):
            total = total + parts[(place + count - owner) % count]
        return total

    sends = [
        [(h, s) for h in range(NZ // 2) for s in range(SUBS) if h < NZ // 2 - 1 or (s < SUBS // 2) == (d == 0)]
        for d in range(2)
    ]
    ring = {}
    received, sent = set(), set()
    neighbours = (device(x, y, c, (z + 1) % NZ), device(x, y, c, (z + NZ - 1) % NZ))

    def ring_copy(d, h, s):
        owner = (z + NZ - h) % NZ if d == 0 else (z + h) % NZ
        part = yb.at[owner, pl.ds(s * SUB, SUB)]
        return pltpu.make_async_remote_copy(
            src_ref=part, dst_ref=part, send_sem=ring_s.at[d, h, s], recv_sem=ring_r.at[d, h, s],
            device_id=neighbours[d], device_id_type=MESH,
        )

    def landed(d, h, s):
        if (d, h, s) not in received:
            received.add((d, h, s))
            ring[d, h, s].wait_recv()

    def left(d, h, s):
        if (d, h, s) not in sent:
            sent.add((d, h, s))
            ring[d, h, s].wait_send()

    done = [0]

    def ticks(count):
        for _ in range(count):
            n = done[0]
            if n >= len(sends[0]):
                return
            for d in range(2):
                h, s = sends[d][n]
                if h > 0:
                    landed(d, h - 1, s)
                if n >= WINDOW:
                    left(d, *sends[d][n - WINDOW])
                ring[d, h, s] = ring_copy(d, h, s)
                ring[d, h, s].start()
            done[0] += 1

    loads[0].wait()
    loads[1].wait()
    q_own = qv[...].T
    for i in range(G):
        r, l = i % 4, i // 4
        width = min(128, OWN - 128 * l)
        if width < 128:
            qst[i] = jnp.zeros((8, 128), F32)
        qst[i, :, :width] = q_own[8 * r : 8 * r + 8, 128 * l : 128 * l + width]
    qz[z] = qst[m]
    t_own = folded(nt(halves(q_own), yb[z]))
    for k in range(NZ):
        r, l = k % 4, k // 4
        tp[k] = t_own[8 * r : 8 * r + 8, 384 * l : 384 * l + 384]
    pl.semaphore_wait(barrier, (NZ - 1) + (NY - 1) + (G - 1))

    t_sums = exchange(0, z_peers, lambda i: tp.at[(z + i) % NZ], lambda i: tr.at[i])
    q_tiles = exchange(1, z_peers, lambda i: qst.at[m], lambda i: qz.at[z])
    ticks(WINDOW)
    rp[...] = jnp.zeros(rp.shape, F32)
    pp[...] = jnp.zeros(pp.shape, F32)
    loads[2].wait()
    xt[...] = xv[...].T
    arrived(t_sums)
    total = tp[z]
    for i in range(1, NZ):
        total = total + tr[i]
    tf[z] = total
    t_parts = exchange(2, z_peers, lambda i: tf.at[z], lambda i: tf.at[z])
    arrived(q_tiles)
    qall[m] = qz[...]
    q_blocks = exchange(3, g_peers, lambda i: qz, lambda i: qall.at[m])
    ticks(2)
    arrived(q_blocks)
    for k in range(NZ):
        for i in range(G):
            r, l = i % 4, i // 4
            width = min(128, OWN - 128 * l)
            qfull[8 * r : 8 * r + 8, OWN * k + 128 * l : OWN * k + 128 * l + width] = qall[i, k, :, :width]
    loads[3].wait()
    p_error = folded(nt(halves(qfull[...]), ev[...]))
    arrived(t_parts)
    t_all = jnp.concatenate(
        [jnp.concatenate([tf[r], tf[r + 4]], axis=1) for r in range(4)], axis=0
    )
    p_own = folded(nn(halves(t_all), xv[...])) + p_error
    for i in range(G):
        x_, c_ = i // 2, i % 2
        width = min(128, ROWS - 128 * x_)
        pp[i, :, :width] = p_own[16 * c_ : 16 * c_ + 16, 128 * x_ : 128 * x_ + width]
    p_sums = exchange(4, g_peers, lambda i: pp.at[(m + i) % G], lambda i: pr.at[i])
    ticks(2)
    arrived(p_sums)
    total = pp[m]
    for i in range(1, G):
        total = total + pr[i]
    py[...] = total
    p_rows = exchange(5, y_peers, lambda i: py, lambda i: pyr.at[i])
    ticks(2)
    arrived(p_rows)
    pyr[0] = py[...]
    pa[m] = in_order(pyr, y, NY)
    p_parts = exchange(6, g_peers, lambda i: pa.at[m], lambda i: pa.at[m])
    ticks(2)
    arrived(p_parts)
    p_all = jnp.concatenate(
        [jnp.concatenate([pa[2 * x_ + c_] for x_ in range(NX)], axis=1) for c_ in range(2)], axis=0
    )[:, :ROWS]
    gram = lax.dot_general(p_all, p_all, (((1,), (1,)), ((), ())), precision=HIGHEST, preferred_element_type=F32)
    for r in range(4):
        gz[:, 32 * r : 32 * r + 32] = gram[8 * r : 8 * r + 8]
    grams = exchange(7, z_peers, lambda i: gz, lambda i: gzr.at[i])
    p_halves = halves(p_all)
    u_halves = halves(folded(nn(p_halves, xt[...])))
    r_error = folded(nn(p_halves, ev[...]))
    ticks(100)
    for d in range(2):
        for h, s in sends[d]:
            landed(d, h, s)
    for k in range(NZ):
        block = folded(nn(u_halves, yb[k])) + r_error[:, OWN * k : OWN * k + OWN]
        for c_ in range(2):
            rp[2 * (k // 2) + c_, :, 256 * (k % 2) : 256 * (k % 2) + OWN] = block[16 * c_ : 16 * c_ + 16]

    def merge(blocks):
        for k in blocks:
            span = slice(OWN * k, OWN * k + OWN)
            mrg[:, span] = nn(xt[...], yb[k]) + ev[:, span].astype(F32)

    r_sums = exchange(8, g_peers, lambda i: rp.at[(m + i) % G], lambda i: rr.at[i])
    merge(range(0, 3))
    arrived(r_sums)
    total = rp[m]
    for i in range(1, G):
        total = total + rr[i]
    for i in range(NY):
        r, l = i % 2, i // 2
        ry[i] = total[8 * r : 8 * r + 8, 128 * l : 128 * l + 128]
    r_rows = exchange(9, y_peers, lambda i: ry.at[(y + i) % NY], lambda i: ryr.at[i])
    arrived(grams)
    gzr[0] = gz[...]
    total = in_order(gzr, z, NZ)
    gram = jnp.concatenate([total[:, 32 * r : 32 * r + 32] for r in range(4)], axis=0)
    inverse = inverse_factor(gram)
    arrived(r_rows)
    total = ry[y]
    for i in range(1, NY):
        total = total + ryr[i]
    rz[...] = total
    r_tiles = exchange(10, z_peers, lambda i: rz, lambda i: rzr.at[i])
    merge(range(3, 6))
    arrived(r_tiles)
    rzr[0] = rz[...]
    rya[y] = in_order(rzr, z, NZ)
    r_back = exchange(11, y_peers, lambda i: rya.at[y], lambda i: rya.at[y])
    merge(range(6, 8))
    p_hat = lax.dot_general(inverse, p_all, (((1,), (0,)), ((), ())), precision=HIGHEST, preferred_element_type=F32)
    p_high = p_hat.astype(BF16)
    p_low = (p_hat - p_high.astype(F32)).astype(BF16)
    p_three = jnp.concatenate([p_high, p_high, p_low], axis=0).T
    arrived(r_back)
    ra[m] = rya[...]
    r_all = exchange(12, g_peers, lambda i: rya, lambda i: ra.at[m])
    arrived(r_all)
    for x_ in range(NX):
        wide = jnp.concatenate(
            [
                jnp.concatenate([ra[2 * x_ + c_, 2 * l + r] for l in range(4)], axis=1)
                for c_ in range(2)
                for r in range(2)
            ],
            axis=0,
        )
        q_wide = lax.dot_general(
            inverse, wide, (((1,), (0,)), ((), ())), precision=HIGHEST, preferred_element_type=F32
        ) * (1.0 / WORKERS)
        for j in range(2):
            k = 2 * x_ + j
            qpad[k] = q_wide[:, 256 * j : 256 * j + 256]
            qnat[:, OWN * k : OWN * k + OWN] = q_wide[:, 256 * j : 256 * j + OWN]
    q_all = qnat[...]
    q_high = q_all.astype(BF16)
    q_low = (q_all - q_high.astype(F32)).astype(BF16)
    q_three = jnp.concatenate([q_high, q_low, q_high], axis=0)
    stores = []
    for i, (first, count) in enumerate([(0, 128), (128, 128), (256, 128), (384, 112)]):
        rows = slice(first, first + count)
        outv[rows, :] = (mrg[rows, :] - nn(p_three[rows], q_three)).astype(BF16)
        store = pltpu.make_async_copy(outv.at[pl.ds(first, count)], out_hbm.at[pl.ds(first, count)], out_sem.at[i])
        store.start()
        stores.append(store)
    qout[...] = qpad[z][:, :OWN].T
    for d in range(2):
        for h, s in sends[d]:
            left(d, h, s)
    for copy in started:
        copy.wait_send()
    for store in stores:
        store.wait()


def on_device(layer_input, output_grad, error_buffer, q_start):
    any_spec = pl.BlockSpec(memory_space=pl.ANY)
    new_error, q_factor = pl.pallas_call(
        kernel,
        out_shape=(jax.ShapeDtypeStruct((ROWS, COLS), BF16), jax.ShapeDtypeStruct((OWN, RANK), F32)),
        in_specs=[any_spec] * 4,
        out_specs=(any_spec, pl.BlockSpec(memory_space=pltpu.VMEM)),
        scratch_shapes=[
            pltpu.VMEM((TOK, ROWS), BF16), pltpu.VMEM((ROWS, TOK), BF16), pltpu.VMEM((NZ, TOK, OWN), BF16),
            pltpu.VMEM((ROWS, COLS), BF16), pltpu.VMEM((OWN, RANK), F32),
            pltpu.VMEM((NZ, 8, 384), F32), pltpu.VMEM((NZ, 8, 384), F32), pltpu.VMEM((NZ, 8, 384), F32),
            pltpu.VMEM((G, 8, 128), F32), pltpu.VMEM((NZ, 8, 128), F32), pltpu.VMEM((G, NZ, 8, 128), F32),
            pltpu.VMEM((RANK, COLS), F32),
            pltpu.VMEM((G, 16, 128), F32), pltpu.VMEM((G, 16, 128), F32), pltpu.VMEM((16, 128), F32),
            pltpu.VMEM((NY, 16, 128), F32), pltpu.VMEM((G, 16, 128), F32),
            pltpu.VMEM((8, 128), F32), pltpu.VMEM((NZ, 8, 128), F32),
            pltpu.VMEM((G, 16, 512), F32), pltpu.VMEM((G, 16, 512), F32), pltpu.VMEM((NY, 8, 128), F32),
            pltpu.VMEM((NY, 8, 128), F32), pltpu.VMEM((8, 128), F32), pltpu.VMEM((NZ, 8, 128), F32),
            pltpu.VMEM((NY, 8, 128), F32), pltpu.VMEM((G, NY, 8, 128), F32),
            pltpu.VMEM((ROWS, COLS), F32), pltpu.VMEM((ROWS, COLS), BF16),
            pltpu.VMEM((NZ, RANK, 256), F32), pltpu.VMEM((RANK, COLS), F32),
            pltpu.SemaphoreType.DMA((4,)), pltpu.SemaphoreType.DMA((4,)),
            pltpu.SemaphoreType.DMA((2, NZ // 2, SUBS)), pltpu.SemaphoreType.DMA((2, NZ // 2, SUBS)),
            pltpu.SemaphoreType.DMA((13, 7)), pltpu.SemaphoreType.DMA((13, 7)),
        ],
        compiler_params=pltpu.CompilerParams(
            collective_id=0, has_side_effects=True, vmem_limit_bytes=48 * 2**20
        ),
    )(layer_input, output_grad, error_buffer[0], q_start)
    return (new_error[None], q_factor)


def solution(mesh):
    return jax.shard_map(
        on_device,
        mesh=mesh,
        in_specs=(P("dp", "shard"), P("dp", "shard"), P("dp", "shard", None), P("shard", None)),
        out_specs=(P("dp", "shard", None), P("shard", None)),
        check_vma=False,
    )
```

```python
import functools

import jax
import jax.numpy as jnp
from jax import lax
from jax.experimental import pallas as pl
from jax.experimental.pallas import tpu as pltpu
from jax.sharding import PartitionSpec as P

MESH = pl.DeviceIdType.MESH
F32, BF16 = jnp.float32, jnp.bfloat16
NX, NY, NZ = 4, 8, 8
G = 2 * NX
TOK, ROWS, COLS, OWN, RANK = 768, 496, 1984, 248, 32
SUBS = 4
SUB = TOK // SUBS
WINDOW = 3
WORKERS = 64
HIGHEST = lax.Precision.HIGHEST


def halves(a):
    high = a.astype(BF16)
    low = (a - high.astype(F32)).astype(BF16)
    return jnp.concatenate([high, low], axis=0)


def folded(a):
    return a[:RANK] + a[RANK:]


def nn(a, b):
    return lax.dot_general(a, b, (((1,), (0,)), ((), ())), preferred_element_type=F32)


def nt(a, b):
    return lax.dot_general(a, b, (((1,), (1,)), ((), ())), preferred_element_type=F32)


def thirds(a):
    high = a.astype(BF16)
    rest = a - high.astype(F32)
    middle = rest.astype(BF16)
    return high, middle, (rest - middle.astype(F32)).astype(BF16)


def product(a, b):
    a0, a1, a2 = thirds(a)
    b0, b1, b2 = thirds(b)
    return nn(jnp.concatenate([a0, a0, a0, a1, a1, a2], axis=1), jnp.concatenate([b0, b1, b2, b0, b1, b0], axis=0))


def inverse_factor(gram):
    row = lax.broadcasted_iota(jnp.int32, (RANK, RANK), 0)
    col = lax.broadcasted_iota(jnp.int32, (RANK, RANK), 1)
    left, right = gram, jnp.where(row == col, 1.0, 0.0).astype(F32)
    index = lax.broadcasted_iota(jnp.int32, (RANK, 1), 0)
    for j in range(RANK):
        scale = 1.0 / jnp.sqrt(left[j : j + 1, j : j + 1])
        left_row, right_row = left[j : j + 1, :] * scale, right[j : j + 1, :] * scale
        column = left[:, j : j + 1] * scale
        below = jnp.where(index > j, column, 0.0)
        left = left - below * left_row
        right = jnp.where(row == j, right_row, right - below * right_row)
    return right


def kernel(
    x_hbm, y_hbm, e_hbm, q_hbm,
    mrg, p_three, q_three, qout,
    xt, yt, yb, ev, qv,
    tp, tr, tf, qst, qz, qall,
    pp, pr, py, pyr, pa,
    gz, gzr,
    up, ur, uf,
    vp, vr, vs, vyr, vz, vzr, va,
    wp, wr, wy, wyr, wa, rs, ra,
    gp, rnat,
    in_sem, ring_s, ring_r, small_s, small_r,
):
    dp, z = lax.axis_index("dp"), lax.axis_index("shard")
    x, y, c = dp // (2 * NY), (dp // 2) % NY, dp % 2
    m = 2 * x + c

    def device(x_, y_, c_, z_):
        return ((x_ * NY + y_) * 2 + c_, z_)

    z_peers = [device(x, y, c, (z + i) % NZ) for i in range(1, NZ)]
    y_peers = [device(x, (y + i) % NY, c, z) for i in range(1, NY)]
    g_peers = [device(((m + i) % G) // 2, y, (m + i) % 2, z) for i in range(1, G)]

    loads = [
        pltpu.make_async_copy(src, dst, in_sem.at[i])
        for i, (src, dst) in enumerate([(y_hbm, yt), (q_hbm, qv), (x_hbm, xt), (e_hbm, ev)])
    ]
    for load in loads:
        load.start()
    barrier = pltpu.get_barrier_semaphore()
    for peer in z_peers + y_peers + g_peers:
        pl.semaphore_signal(barrier, inc=1, device_id=peer, device_id_type=MESH)

    started = []

    def exchange(stage, peers, src, dst):
        copies = {}
        for i in far_first(peers):
            copy = pltpu.make_async_remote_copy(
                src_ref=src(i), dst_ref=dst(i), send_sem=small_s.at[stage, i - 1], recv_sem=small_r.at[stage, i - 1],
                device_id=peers[i - 1], device_id_type=MESH,
            )
            copy.start()
            copies[i] = copy
        if len(started) > 1:
            for copy in started.pop(0).values():
                copy.wait_send()
        started.append(copies)
        return copies

    def far_first(peers):
        places = range(1, len(peers) + 1)
        return sorted(places, key=lambda i: -min(i, len(peers) + 1 - i))

    def arrived(copies, between=0):
        order = far_first(copies)[::-1]
        for i in order[:4]:
            copies[i].wait_recv()
        ticks(between)
        for i in order[4:]:
            copies[i].wait_recv()

    def in_order(parts, place, count):
        total = parts[place]
        for owner in range(1, count):
            total = total + parts[(place + count - owner) % count]
        return total

    def cut(a, tile):
        for i in range(G):
            r, l = i % 4, i // 4
            width = min(128, OWN - 128 * l)
            piece = a[8 * r : 8 * r + 8, 128 * l : 128 * l + width]
            tile(i)[...] = piece if width == 128 else jnp.pad(piece, ((0, 0), (0, 128 - width)))

    def uncut(tiles, out):
        for k in range(NZ):
            for i in range(G):
                r, l = i % 4, i // 4
                width = min(128, OWN - 128 * l)
                start = OWN * k + 128 * l
                out[8 * r : 8 * r + 8, start : start + width] = tiles[i, k, :, :width]

    def spread(a, parts):
        for k in range(NZ):
            r, l = k % 4, k // 4
            parts[k] = a[8 * r : 8 * r + 8, 384 * l : 384 * l + 384]

    def gathered(parts):
        return jnp.concatenate([jnp.concatenate([parts[r], parts[r + 4]], axis=1) for r in range(4)], axis=0)

    def summed(own, parts, count):
        total = own
        for i in range(1, count):
            total = total + parts[i]
        return total

    sends = [
        [(h, s) for h in range(NZ // 2) for s in range(SUBS) if h < NZ // 2 - 1 or (s < SUBS // 2) == (d == 0)]
        for d in range(2)
    ]
    ring = {}
    received, sent = set(), set()
    neighbours = (device(x, y, c, (z + 1) % NZ), device(x, y, c, (z + NZ - 1) % NZ))

    def ring_copy(d, h, s):
        owner = (z + NZ - h) % NZ if d == 0 else (z + h) % NZ
        part = yb.at[owner, pl.ds(s * SUB, SUB)]
        return pltpu.make_async_remote_copy(
            src_ref=part, dst_ref=part, send_sem=ring_s.at[d, h, s], recv_sem=ring_r.at[d, h, s],
            device_id=neighbours[d], device_id_type=MESH,
        )

    def landed(d, h, s):
        if (d, h, s) not in received:
            received.add((d, h, s))
            ring[d, h, s].wait_recv()

    def gone(d, h, s):
        if (d, h, s) not in sent:
            sent.add((d, h, s))
            ring[d, h, s].wait_send()

    done = [0]

    def ticks(count):
        for _ in range(count):
            n = done[0]
            if n >= len(sends[0]):
                return
            for d in range(2):
                h, s = sends[d][n]
                if h > 0:
                    landed(d, h - 1, s)
                if n >= WINDOW:
                    gone(d, *sends[d][n - WINDOW])
                ring[d, h, s] = ring_copy(d, h, s)
                ring[d, h, s].start()
            done[0] += 1

    loads[0].wait()
    loads[1].wait()
    q_own = qv[...]
    yb[z] = yt[...].T
    cut(q_own, lambda i: qst.at[i])
    qz[z] = qst[m]
    t_own = folded(nn(halves(q_own), yt[...]))
    spread(t_own, tp)
    pl.semaphore_wait(barrier, (NZ - 1) + (NY - 1) + (G - 1))

    q_tiles = exchange(0, z_peers, lambda i: qst.at[m], lambda i: qz.at[z])
    t_sums = exchange(1, z_peers, lambda i: tp.at[(z + i) % NZ], lambda i: tr.at[i])
    ticks(2)
    pp[...] = jnp.zeros(pp.shape, F32)
    loads[2].wait()
    arrived(q_tiles)
    qall[m] = qz[...]
    q_blocks = exchange(2, g_peers, lambda i: qz, lambda i: qall.at[m])
    arrived(t_sums)
    tf[z] = summed(tp[z], tr, NZ)
    t_parts = exchange(3, z_peers, lambda i: tf.at[z], lambda i: tf.at[z])
    ticks(2)
    loads[3].wait()
    arrived(q_blocks)
    uncut(qall, rnat)
    p_error = folded(nt(halves(rnat[...]), ev[...]))
    arrived(t_parts)
    p_own = folded(nt(halves(gathered(tf)), xt[...])) + p_error
    for i in range(G):
        x_, c_ = i // 2, i % 2
        width = min(128, ROWS - 128 * x_)
        pp[i, :, :width] = p_own[16 * c_ : 16 * c_ + 16, 128 * x_ : 128 * x_ + width]

    p_sums = exchange(4, g_peers, lambda i: pp.at[(m + i) % G], lambda i: pr.at[i])
    ticks(2)
    arrived(p_sums)
    py[...] = summed(pp[m], pr, G)
    p_rows = exchange(5, y_peers, lambda i: py, lambda i: pyr.at[i])
    ticks(2)
    arrived(p_rows)
    pyr[0] = py[...]
    pa[m] = in_order(pyr, y, NY)
    p_parts = exchange(6, g_peers, lambda i: pa.at[m], lambda i: pa.at[m])
    ticks(2)
    arrived(p_parts)
    p_all = jnp.concatenate(
        [jnp.concatenate([pa[2 * x_ + c_] for x_ in range(NX)], axis=1) for c_ in range(2)], axis=0
    )[:, :ROWS]

    p_halves = halves(p_all)
    spread(folded(nn(p_halves, xt[...])), up)
    u_sums = exchange(7, z_peers, lambda i: up.at[(z + i) % NZ], lambda i: ur.at[i])
    v_own = folded(nn(p_halves, ev[...]))
    for k in range(NZ):
        cut(v_own[:, OWN * k : OWN * k + OWN], lambda i: vp.at[i, k])
    v_sums = exchange(8, g_peers, lambda i: vp.at[(m + i) % G], lambda i: vr.at[i])
    ticks(1)
    gram = lax.dot_general(p_all, p_all, (((1,), (1,)), ((), ())), precision=HIGHEST, preferred_element_type=F32)
    for r in range(4):
        gz[:, 32 * r : 32 * r + 32] = gram[8 * r : 8 * r + 8]
    arrived(u_sums)
    uf[z] = summed(up[z], ur, NZ)
    u_parts = exchange(9, z_peers, lambda i: uf.at[z], lambda i: uf.at[z])
    grams = exchange(10, z_peers, lambda i: gz, lambda i: gzr.at[i])
    arrived(v_sums)
    vs[...] = summed(vp[m], vr, G)
    v_rows = exchange(11, y_peers, lambda i: vs.at[(y + i) % NY], lambda i: vyr.at[i])
    ticks(2)
    arrived(u_parts)
    w_own = folded(nn(halves(gathered(uf)), yb[z]))
    cut(w_own, lambda i: wp.at[i])
    w_sums = exchange(12, g_peers, lambda i: wp.at[(m + i) % G], lambda i: wr.at[i])
    arrived(v_rows)
    vz[...] = summed(vs[y], vyr, NY)
    v_tiles = exchange(13, z_peers, lambda i: vz, lambda i: vzr.at[i])
    ticks(100)
    arrived(w_sums)
    wy[...] = summed(wp[m], wr, G)
    w_rows = exchange(14, y_peers, lambda i: wy, lambda i: wyr.at[i])
    arrived(grams)
    gzr[0] = gz[...]
    total = in_order(gzr, z, NZ)
    gram = jnp.concatenate([total[:, 32 * r : 32 * r + 32] for r in range(4)], axis=0)
    inverse = inverse_factor(gram)
    arrived(w_rows)
    wyr[0] = wy[...]
    wa[z] = in_order(wyr, y, NY)
    w_tiles = exchange(15, z_peers, lambda i: wa.at[z], lambda i: wa.at[z])
    arrived(v_tiles)
    vzr[0] = vz[...]
    va[y] = in_order(vzr, z, NZ)
    v_back = exchange(16, y_peers, lambda i: va.at[y], lambda i: va.at[y])
    for d in range(2):
        for h, s in sends[d]:
            landed(d, h, s)

    def gradient(k, carry):
        gp[k] = nn(xt[...], yb[k])
        return carry

    def merge(i, carry):
        rows = pl.ds(pl.multiple_of(16 * i, 16), 16)
        for k in range(NZ):
            span = slice(OWN * k, OWN * k + OWN)
            mrg[rows, span] = gp[k, rows, :] + ev[rows, span].astype(F32)
        return carry

    lax.fori_loop(0, NZ, gradient, 0)
    arrived(w_tiles)
    arrived(v_back)
    rs[...] = wa[...] + va[...]
    ra[m] = rs[...]
    r_all = exchange(17, g_peers, lambda i: rs, lambda i: ra.at[m])
    lax.fori_loop(0, ROWS // 16, merge, 0)
    p_hat = product(inverse, p_all)
    p_high = p_hat.astype(BF16)
    p_low = (p_hat - p_high.astype(F32)).astype(BF16)
    p_three[...] = jnp.concatenate([p_high, p_high, p_low], axis=0).T
    for d in range(2):
        for h, s in sends[d]:
            gone(d, h, s)
    arrived(r_all)
    uncut(ra, rnat)
    q_all = product(inverse, rnat[...]) * (1.0 / WORKERS)
    q_high = q_all.astype(BF16)
    q_low = (q_all - q_high.astype(F32)).astype(BF16)
    q_three[...] = jnp.concatenate([q_high, q_low, q_high], axis=0)
    r_own = jnp.concatenate([jnp.concatenate([ra[r, z], ra[r + 4, z]], axis=1) for r in range(4)], axis=0)
    qout[...] = (product(inverse, r_own) * (1.0 / WORKERS))[:, :OWN]
    for copies in started:
        for copy in copies.values():
            copy.wait_send()


def finish(mrg, p_three, q_three, q_own, out_hbm, q_out, outv, out_sem):
    stores = [pltpu.make_async_copy(q_own, q_out, out_sem.at[4])]
    stores[0].start()
    for i, (first, count) in enumerate([(0, 128), (128, 128), (256, 128), (384, 112)]):
        rows = slice(first, first + count)
        outv[rows, :] = (mrg[rows, :] - nn(p_three[rows, :], q_three[...])).astype(BF16)
        store = pltpu.make_async_copy(outv.at[pl.ds(first, count)], out_hbm.at[pl.ds(first, count)], out_sem.at[i])
        store.start()
        stores.append(store)
    for store in stores:
        store.wait()


def on_device(layer_input, output_grad, error_buffer, q_start):
    hbm, vmem = pl.BlockSpec(memory_space=pltpu.HBM), pl.BlockSpec(memory_space=pltpu.VMEM)
    merged, p_three, q_three, q_own = pl.pallas_call(
        kernel,
        out_shape=(
            jax.ShapeDtypeStruct((ROWS, COLS), F32), jax.ShapeDtypeStruct((ROWS, 3 * RANK), BF16),
            jax.ShapeDtypeStruct((3 * RANK, COLS), BF16), jax.ShapeDtypeStruct((RANK, OWN), F32),
        ),
        in_specs=[hbm] * 4,
        out_specs=(vmem,) * 4,
        scratch_shapes=[
            pltpu.VMEM((ROWS, TOK), BF16), pltpu.VMEM((OWN, TOK), BF16), pltpu.VMEM((NZ, TOK, OWN), BF16),
            pltpu.VMEM((ROWS, COLS), BF16), pltpu.VMEM((RANK, OWN), F32),
            pltpu.VMEM((NZ, 8, 384), F32), pltpu.VMEM((NZ, 8, 384), F32), pltpu.VMEM((NZ, 8, 384), F32),
            pltpu.VMEM((G, 8, 128), F32), pltpu.VMEM((NZ, 8, 128), F32), pltpu.VMEM((G, NZ, 8, 128), F32),
            pltpu.VMEM((G, 16, 128), F32), pltpu.VMEM((G, 16, 128), F32), pltpu.VMEM((16, 128), F32),
            pltpu.VMEM((NY, 16, 128), F32), pltpu.VMEM((G, 16, 128), F32),
            pltpu.VMEM((8, 128), F32), pltpu.VMEM((NZ, 8, 128), F32),
            pltpu.VMEM((NZ, 8, 384), F32), pltpu.VMEM((NZ, 8, 384), F32), pltpu.VMEM((NZ, 8, 384), F32),
            pltpu.VMEM((G, NZ, 8, 128), F32), pltpu.VMEM((G, NZ, 8, 128), F32), pltpu.VMEM((NZ, 8, 128), F32),
            pltpu.VMEM((NY, 8, 128), F32), pltpu.VMEM((8, 128), F32), pltpu.VMEM((NZ, 8, 128), F32),
            pltpu.VMEM((NY, 8, 128), F32),
            pltpu.VMEM((G, 8, 128), F32), pltpu.VMEM((G, 8, 128), F32), pltpu.VMEM((8, 128), F32),
            pltpu.VMEM((NY, 8, 128), F32), pltpu.VMEM((NZ, 8, 128), F32), pltpu.VMEM((NZ, 8, 128), F32),
            pltpu.VMEM((G, NZ, 8, 128), F32),
            pltpu.VMEM((NZ, ROWS, OWN), F32), pltpu.VMEM((RANK, COLS), F32),
            pltpu.SemaphoreType.DMA((4,)),
            pltpu.SemaphoreType.DMA((2, NZ // 2, SUBS)), pltpu.SemaphoreType.DMA((2, NZ // 2, SUBS)),
            pltpu.SemaphoreType.DMA((18, 7)), pltpu.SemaphoreType.DMA((18, 7)),
        ],
        compiler_params=pltpu.CompilerParams(
            collective_id=0, has_side_effects=True, vmem_limit_bytes=40 * 2**20
        ),
    )(*(
        pltpu.with_memory_space_constraint(a, pltpu.HBM)
        for a in (layer_input.T, output_grad.T, error_buffer[0], q_start.T)
    ))
    new_error, q_factor = pl.pallas_call(
        finish,
        out_shape=(jax.ShapeDtypeStruct((ROWS, COLS), BF16), jax.ShapeDtypeStruct((RANK, OWN), F32)),
        in_specs=[vmem] * 4,
        out_specs=(hbm, hbm),
        scratch_shapes=[pltpu.VMEM((ROWS, COLS), BF16), pltpu.SemaphoreType.DMA((5,))],
        compiler_params=pltpu.CompilerParams(vmem_limit_bytes=16 * 2**20),
    )(merged, p_three, q_three, q_own)
    return (new_error[None], q_factor.T)


def solution(mesh):
    return jax.shard_map(
        on_device,
        mesh=mesh,
        in_specs=(P("dp", "shard"), P("dp", "shard"), P("dp", "shard", None), P("shard", None)),
        out_specs=(P("dp", "shard", None), P("shard", None)),
        check_vma=False,
    )
```

```python
import functools

import jax
import jax.numpy as jnp
from jax import lax
from jax.experimental import pallas as pl
from jax.experimental.pallas import tpu as pltpu
from jax.sharding import PartitionSpec as P

MESH = pl.DeviceIdType.MESH
F32, BF16 = jnp.float32, jnp.bfloat16
NX, NY, NZ = 4, 8, 8
G = 2 * NX
TOK, ROWS, COLS, OWN, RANK = 768, 496, 1984, 248, 32
SUBS = 4
SUB = TOK // SUBS
WORKERS = 64
HIGHEST = lax.Precision.HIGHEST


def halves(a):
    high = a.astype(BF16)
    low = (a - high.astype(F32)).astype(BF16)
    return jnp.concatenate([high, low], axis=0)


def folded(a):
    return a[:RANK] + a[RANK:]


def nn(a, b):
    return lax.dot_general(a, b, (((1,), (0,)), ((), ())), preferred_element_type=F32)


def nt(a, b):
    return lax.dot_general(a, b, (((1,), (1,)), ((), ())), preferred_element_type=F32)


def thirds(a):
    high = a.astype(BF16)
    rest = a - high.astype(F32)
    middle = rest.astype(BF16)
    return high, middle, (rest - middle.astype(F32)).astype(BF16)


def product(a, b):
    a0, a1, a2 = thirds(a)
    b0, b1, b2 = thirds(b)
    return nn(jnp.concatenate([a0, a0, a0, a1, a1, a2], axis=1), jnp.concatenate([b0, b1, b2, b0, b1, b0], axis=0))


def inverse_factor(gram):
    row = lax.broadcasted_iota(jnp.int32, (RANK, RANK), 0)
    col = lax.broadcasted_iota(jnp.int32, (RANK, RANK), 1)
    left, right = gram, jnp.where(row == col, 1.0, 0.0).astype(F32)
    index = lax.broadcasted_iota(jnp.int32, (RANK, 1), 0)
    for j in range(RANK):
        scale = 1.0 / jnp.sqrt(left[j : j + 1, j : j + 1])
        left_row, right_row = left[j : j + 1, :] * scale, right[j : j + 1, :] * scale
        column = left[:, j : j + 1] * scale
        below = jnp.where(index > j, column, 0.0)
        left = left - below * left_row
        right = jnp.where(row == j, right_row, right - below * right_row)
    return right


def kernel(
    x_hbm, y_hbm, e_hbm, q_hbm,
    mrg, b_three, r_three, r_own, inverse_out,
    xt, yt, yb, ev, qv,
    tp, tr, tf, qst, qz, qall,
    pp, pr, py, pyr, pa,
    gz, gzr,
    up, ur, uf,
    vp, vr, vs, vyr, vz, vzr, va,
    wp, wr, wy, wyr, wa, rs, ra,
    gp, rnat,
    in_sem, ring_s, ring_r, small_s, small_r,
):
    dp, z = lax.axis_index("dp"), lax.axis_index("shard")
    x, y, c = dp // (2 * NY), (dp // 2) % NY, dp % 2
    m = 2 * x + c

    def device(x_, y_, c_, z_):
        return ((x_ * NY + y_) * 2 + c_, z_)

    z_peers = [device(x, y, c, (z + i) % NZ) for i in range(1, NZ)]
    y_peers = [device(x, (y + i) % NY, c, z) for i in range(1, NY)]
    g_peers = [device(((m + i) % G) // 2, y, (m + i) % 2, z) for i in range(1, G)]

    loads = [
        pltpu.make_async_copy(src, dst, in_sem.at[i])
        for i, (src, dst) in enumerate([(y_hbm, yt), (q_hbm, qv), (x_hbm, xt), (e_hbm, ev)])
    ]
    for load in loads:
        load.start()
    barrier = pltpu.get_barrier_semaphore()
    for peer in z_peers + y_peers + g_peers:
        pl.semaphore_signal(barrier, inc=1, device_id=peer, device_id_type=MESH)

    def far_first(peers):
        places = range(1, len(peers) + 1)
        return sorted(places, key=lambda i: -min(i, len(peers) + 1 - i))

    stages = {}

    def exchange(stage, peers, src, dst, buffer):
        for i in far_first(peers):
            pltpu.make_async_remote_copy(
                src_ref=src(i), dst_ref=dst(i), send_sem=small_s.at[stage], recv_sem=small_r.at[stage],
                device_id=peers[i - 1], device_id_type=MESH,
            ).start()
        stages[stage] = buffer.at[pl.ds(1, len(peers))]
        return stage

    def arrived(stage):
        pltpu.make_async_copy(stages[stage], stages[stage], small_r.at[stage]).wait()

    def all_sent():
        for stage, pieces in stages.items():
            pltpu.make_async_copy(pieces, pieces, small_s.at[stage]).wait()
        pieces = yb.at[pl.ds(0, NZ - 1)]
        pltpu.make_async_copy(pieces, pieces, ring_s.at[0]).wait()

    def in_order(parts, place, count):
        total = parts[place]
        for owner in range(1, count):
            total = total + parts[(place + count - owner) % count]
        return total

    def cut(a, tile):
        for i in range(G):
            r, l = i % 4, i // 4
            width = min(128, OWN - 128 * l)
            piece = a[8 * r : 8 * r + 8, 128 * l : 128 * l + width]
            tile(i)[...] = piece if width == 128 else jnp.pad(piece, ((0, 0), (0, 128 - width)))

    def uncut(tiles, out):
        for k in range(NZ):
            for i in range(G):
                r, l = i % 4, i // 4
                width = min(128, OWN - 128 * l)
                start = OWN * k + 128 * l
                out[8 * r : 8 * r + 8, start : start + width] = tiles[i, k, :, :width]

    def spread(a, parts):
        for k in range(NZ):
            r, l = k % 4, k // 4
            parts[k] = a[8 * r : 8 * r + 8, 384 * l : 384 * l + 384]

    def gathered(parts):
        return jnp.concatenate([jnp.concatenate([parts[r], parts[r + 4]], axis=1) for r in range(4)], axis=0)

    def summed(own, parts, count):
        total = own
        for i in range(1, count):
            total = total + parts[i]
        return total

    sends = [
        [(h, s) for h in range(NZ // 2) for s in range(SUBS) if h < NZ // 2 - 1 or (s < SUBS // 2) == (d == 0)]
        for d in range(2)
    ]
    ring = {}
    received = set()
    neighbours = (device(x, y, c, (z + 1) % NZ), device(x, y, c, (z + NZ - 1) % NZ))

    def ring_copy(d, h, s):
        owner = (z + NZ - h) % NZ if d == 0 else (z + h) % NZ
        part = yb.at[owner, pl.ds(s * SUB, SUB)]
        return pltpu.make_async_remote_copy(
            src_ref=part, dst_ref=part, send_sem=ring_s.at[0], recv_sem=ring_r.at[d, h, s],
            device_id=neighbours[d], device_id_type=MESH,
        )

    def landed(d, h, s):
        if (d, h, s) not in received:
            received.add((d, h, s))
            ring[d, h, s].wait_recv()

    done = [0]

    def ticks(count):
        for _ in range(count):
            n = done[0]
            if n >= len(sends[0]):
                return
            for d in range(2):
                h, s = sends[d][n]
                if h > 0:
                    landed(d, h - 1, s)
                ring[d, h, s] = ring_copy(d, h, s)
                ring[d, h, s].start()
            done[0] += 1

    loads[0].wait()
    loads[1].wait()
    q_own = qv[...]
    cut(q_own, lambda i: qst.at[i])
    qz[z] = qst[m]
    t_own = folded(nn(halves(q_own), yt[...]))
    spread(t_own, tp)
    pl.semaphore_wait(barrier, (NZ - 1) + (NY - 1) + (G - 1))

    q_tiles = exchange(0, z_peers, lambda i: qst.at[m], lambda i: qz.at[z], qz)
    t_sums = exchange(1, z_peers, lambda i: tp.at[(z + i) % NZ], lambda i: tr.at[i], tr)
    yb[z] = yt[...].T
    ticks(1)
    arrived(q_tiles)
    qall[m] = qz[...]
    q_blocks = exchange(2, g_peers, lambda i: qz, lambda i: qall.at[m], qall)
    arrived(t_sums)
    tf[z] = summed(tp[z], tr, NZ)
    t_parts = exchange(3, z_peers, lambda i: tf.at[z], lambda i: tf.at[z], tf)
    ticks(2)
    pp[...] = jnp.zeros(pp.shape, F32)
    loads[2].wait()
    loads[3].wait()
    arrived(q_blocks)
    uncut(qall, rnat)
    p_error = folded(nt(halves(rnat[...]), ev[...]))
    arrived(t_parts)
    p_own = folded(nt(halves(gathered(tf)), xt[...])) + p_error
    for i in range(G):
        x_, c_ = i // 2, i % 2
        width = min(128, ROWS - 128 * x_)
        pp[i, :, :width] = p_own[16 * c_ : 16 * c_ + 16, 128 * x_ : 128 * x_ + width]

    p_sums = exchange(4, g_peers, lambda i: pp.at[(m + i) % G], lambda i: pr.at[i], pr)
    ticks(2)
    arrived(p_sums)
    py[...] = summed(pp[m], pr, G)
    p_rows = exchange(5, y_peers, lambda i: py, lambda i: pyr.at[i], pyr)
    ticks(2)
    arrived(p_rows)
    pyr[0] = py[...]
    pa[m] = in_order(pyr, y, NY)
    p_parts = exchange(6, g_peers, lambda i: pa.at[m], lambda i: pa.at[m], pa)
    ticks(2)
    arrived(p_parts)
    p_all = jnp.concatenate(
        [jnp.concatenate([pa[2 * x_ + c_] for x_ in range(NX)], axis=1) for c_ in range(2)], axis=0
    )[:, :ROWS]

    def gradients(first, count):
        def one(i, carry):
            owner = (z + first + i) % NZ
            gp[owner] = nn(xt[...], yb[owner])
            return carry

        lax.fori_loop(0, count, one, 0)

    def landed_steps(steps):
        for d in range(2):
            for h, s in sends[d]:
                if h in steps:
                    landed(d, h, s)

    p_halves = halves(p_all)
    spread(folded(nn(p_halves, xt[...])), up)
    u_sums = exchange(7, z_peers, lambda i: up.at[(z + i) % NZ], lambda i: ur.at[i], ur)
    v_own = folded(nn(p_halves, ev[...]))
    for k in range(NZ):
        cut(v_own[:, OWN * k : OWN * k + OWN], lambda i: vp.at[i, k])
    v_sums = exchange(8, g_peers, lambda i: vp.at[(m + i) % G], lambda i: vr.at[i], vr)
    ticks(2)
    arrived(u_sums)
    uf[z] = summed(up[z], ur, NZ)
    u_parts = exchange(9, z_peers, lambda i: uf.at[z], lambda i: uf.at[z], uf)
    gram = lax.dot_general(p_all, p_all, (((1,), (1,)), ((), ())), precision=HIGHEST, preferred_element_type=F32)
    for r in range(4):
        gz[:, 32 * r : 32 * r + 32] = gram[8 * r : 8 * r + 8]
    grams = exchange(10, z_peers, lambda i: gz, lambda i: gzr.at[i], gzr)
    arrived(v_sums)
    vs[...] = summed(vp[m], vr, G)
    v_rows = exchange(11, y_peers, lambda i: vs.at[(y + i) % NY], lambda i: vyr.at[i], vyr)
    ticks(2)
    arrived(u_parts)
    w_own = folded(nn(halves(gathered(uf)), yb[z]))
    cut(w_own, lambda i: wp.at[i])
    w_sums = exchange(12, g_peers, lambda i: wp.at[(m + i) % G], lambda i: wr.at[i], wr)
    arrived(v_rows)
    vz[...] = summed(vs[y], vyr, NY)
    v_tiles = exchange(13, z_peers, lambda i: vz, lambda i: vzr.at[i], vzr)
    ticks(100)
    arrived(grams)
    gzr[0] = gz[...]
    total = in_order(gzr, z, NZ)
    gram = jnp.concatenate([total[:, 32 * r : 32 * r + 32] for r in range(4)], axis=0)
    inverse = inverse_factor(gram)
    arrived(w_sums)
    wy[...] = summed(wp[m], wr, G)
    w_rows = exchange(14, y_peers, lambda i: wy, lambda i: wyr.at[i], wyr)
    landed_steps((0, 1))
    gradients(6, 5)
    arrived(w_rows)
    wyr[0] = wy[...]
    wa[z] = in_order(wyr, y, NY)
    w_tiles = exchange(15, z_peers, lambda i: wa.at[z], lambda i: wa.at[z], wa)
    arrived(v_tiles)
    vzr[0] = vz[...]
    va[y] = in_order(vzr, z, NZ)
    v_back = exchange(16, y_peers, lambda i: va.at[y], lambda i: va.at[y], va)
    landed_steps((2, 3))

    def merge(i, carry):
        rows = pl.ds(pl.multiple_of(16 * i, 16), 16)
        for k in range(NZ):
            span = slice(OWN * k, OWN * k + OWN)
            mrg[rows, span] = gp[k, rows, :] + ev[rows, span].astype(F32)
        return carry

    gradients(3, 3)
    arrived(w_tiles)
    arrived(v_back)
    rs[...] = wa[...] + va[...]
    ra[m] = rs[...]
    r_all = exchange(17, g_peers, lambda i: rs, lambda i: ra.at[m], ra)
    lax.fori_loop(0, ROWS // 16, merge, 0)
    p_hat = product(inverse, p_all)
    b = product(inverse.T, p_hat) * (1.0 / WORKERS)
    b_high = b.astype(BF16)
    b_low = (b - b_high.astype(F32)).astype(BF16)
    b_three[...] = jnp.concatenate([b_high, b_high, b_low], axis=0).T
    inverse_out[...] = inverse
    arrived(r_all)
    uncut(ra, rnat)
    r_all = rnat[...]
    r_high = r_all.astype(BF16)
    r_low = (r_all - r_high.astype(F32)).astype(BF16)
    r_three[...] = jnp.concatenate([r_high, r_low, r_high], axis=0)
    r_own[...] = jnp.concatenate([jnp.concatenate([ra[r, z], ra[r + 4, z]], axis=1) for r in range(4)], axis=0)
    all_sent()


def finish(mrg, b_three, r_three, r_own, inverse, out_hbm, q_out, outv, q_own, out_sem):
    stores = []
    for i, (first, count) in enumerate([(0, 128), (128, 128), (256, 128), (384, 112)]):
        rows = slice(first, first + count)
        outv[rows, :] = (mrg[rows, :] - nn(b_three[rows, :], r_three[...])).astype(BF16)
        store = pltpu.make_async_copy(outv.at[pl.ds(first, count)], out_hbm.at[pl.ds(first, count)], out_sem.at[i])
        store.start()
        stores.append(store)
    q_own[...] = (product(inverse[...], r_own[...]) * (1.0 / WORKERS))[:, :OWN]
    stores.append(pltpu.make_async_copy(q_own, q_out, out_sem.at[4]))
    stores[-1].start()
    for store in stores:
        store.wait()


def on_device(layer_input, output_grad, error_buffer, q_start):
    hbm, vmem = pl.BlockSpec(memory_space=pltpu.HBM), pl.BlockSpec(memory_space=pltpu.VMEM)
    merged, b_three, r_three, r_own, inverse = pl.pallas_call(
        kernel,
        out_shape=(
            jax.ShapeDtypeStruct((ROWS, COLS), F32), jax.ShapeDtypeStruct((ROWS, 3 * RANK), BF16),
            jax.ShapeDtypeStruct((3 * RANK, COLS), BF16), jax.ShapeDtypeStruct((RANK, 256), F32),
            jax.ShapeDtypeStruct((RANK, RANK), F32),
        ),
        in_specs=[hbm] * 4,
        out_specs=(vmem,) * 5,
        scratch_shapes=[
            pltpu.VMEM((ROWS, TOK), BF16), pltpu.VMEM((OWN, TOK), BF16), pltpu.VMEM((NZ, TOK, OWN), BF16),
            pltpu.VMEM((ROWS, COLS), BF16), pltpu.VMEM((RANK, OWN), F32),
            pltpu.VMEM((NZ, 8, 384), F32), pltpu.VMEM((NZ, 8, 384), F32), pltpu.VMEM((NZ, 8, 384), F32),
            pltpu.VMEM((G, 8, 128), F32), pltpu.VMEM((NZ, 8, 128), F32), pltpu.VMEM((G, NZ, 8, 128), F32),
            pltpu.VMEM((G, 16, 128), F32), pltpu.VMEM((G, 16, 128), F32), pltpu.VMEM((16, 128), F32),
            pltpu.VMEM((NY, 16, 128), F32), pltpu.VMEM((G, 16, 128), F32),
            pltpu.VMEM((8, 128), F32), pltpu.VMEM((NZ, 8, 128), F32),
            pltpu.VMEM((NZ, 8, 384), F32), pltpu.VMEM((NZ, 8, 384), F32), pltpu.VMEM((NZ, 8, 384), F32),
            pltpu.VMEM((G, NZ, 8, 128), F32), pltpu.VMEM((G, NZ, 8, 128), F32), pltpu.VMEM((NZ, 8, 128), F32),
            pltpu.VMEM((NY, 8, 128), F32), pltpu.VMEM((8, 128), F32), pltpu.VMEM((NZ, 8, 128), F32),
            pltpu.VMEM((NY, 8, 128), F32),
            pltpu.VMEM((G, 8, 128), F32), pltpu.VMEM((G, 8, 128), F32), pltpu.VMEM((8, 128), F32),
            pltpu.VMEM((NY, 8, 128), F32), pltpu.VMEM((NZ, 8, 128), F32), pltpu.VMEM((NZ, 8, 128), F32),
            pltpu.VMEM((G, NZ, 8, 128), F32),
            pltpu.VMEM((NZ, ROWS, OWN), F32), pltpu.VMEM((RANK, COLS), F32),
            pltpu.SemaphoreType.DMA((4,)),
            pltpu.SemaphoreType.DMA((1,)), pltpu.SemaphoreType.DMA((2, NZ // 2, SUBS)),
            pltpu.SemaphoreType.DMA((18,)), pltpu.SemaphoreType.DMA((18,)),
        ],
        compiler_params=pltpu.CompilerParams(
            collective_id=0, has_side_effects=True, vmem_limit_bytes=40 * 2**20
        ),
    )(*(
        pltpu.with_memory_space_constraint(a, pltpu.HBM)
        for a in (layer_input.T, output_grad.T, error_buffer[0], q_start.T)
    ))
    new_error, q_factor = pl.pallas_call(
        finish,
        out_shape=(jax.ShapeDtypeStruct((ROWS, COLS), BF16), jax.ShapeDtypeStruct((RANK, OWN), F32)),
        in_specs=[vmem] * 5,
        out_specs=(hbm, hbm),
        scratch_shapes=[pltpu.VMEM((ROWS, COLS), BF16), pltpu.VMEM((RANK, OWN), F32), pltpu.SemaphoreType.DMA((5,))],
        compiler_params=pltpu.CompilerParams(vmem_limit_bytes=16 * 2**20),
    )(merged, b_three, r_three, r_own, inverse)
    return (new_error[None], q_factor.T)


def solution(mesh):
    return jax.shard_map(
        on_device,
        mesh=mesh,
        in_specs=(P("dp", "shard"), P("dp", "shard"), P("dp", "shard", None), P("shard", None)),
        out_specs=(P("dp", "shard", None), P("shard", None)),
        check_vma=False,
    )
```

```python
import functools

import jax
import jax.numpy as jnp
from jax import lax
from jax.experimental import pallas as pl
from jax.experimental.pallas import tpu as pltpu
from jax.sharding import PartitionSpec as P

MESH = pl.DeviceIdType.MESH
F32, BF16 = jnp.float32, jnp.bfloat16
NX, NY, NZ = 4, 8, 8
G = 2 * NX
TOK, ROWS, COLS, OWN, RANK = 768, 496, 1984, 248, 32
SUBS = 4
SUB = TOK // SUBS
WORKERS = 64
HIGHEST = lax.Precision.HIGHEST


def halves(a):
    high = a.astype(BF16)
    low = (a - high.astype(F32)).astype(BF16)
    return jnp.concatenate([high, low], axis=0)


def folded(a):
    return a[:RANK] + a[RANK:]


def nn(a, b):
    return lax.dot_general(a, b, (((1,), (0,)), ((), ())), preferred_element_type=F32)


def nt(a, b):
    return lax.dot_general(a, b, (((1,), (1,)), ((), ())), preferred_element_type=F32)


def thirds(a):
    high = a.astype(BF16)
    rest = a - high.astype(F32)
    middle = rest.astype(BF16)
    return high, middle, (rest - middle.astype(F32)).astype(BF16)


def product(a, b):
    a0, a1, a2 = thirds(a)
    b0, b1, b2 = thirds(b)
    return nn(jnp.concatenate([a0, a0, a0, a1, a1, a2], axis=1), jnp.concatenate([b0, b1, b2, b0, b1, b0], axis=0))


def inverse_factor(gram):
    row = lax.broadcasted_iota(jnp.int32, (RANK, RANK), 0)
    col = lax.broadcasted_iota(jnp.int32, (RANK, RANK), 1)
    left, right = gram, jnp.where(row == col, 1.0, 0.0).astype(F32)
    index = lax.broadcasted_iota(jnp.int32, (RANK, 1), 0)
    for j in range(RANK):
        scale = 1.0 / jnp.sqrt(left[j : j + 1, j : j + 1])
        left_row, right_row = left[j : j + 1, :] * scale, right[j : j + 1, :] * scale
        column = left[:, j : j + 1] * scale
        below = jnp.where(index > j, column, 0.0)
        left = left - below * left_row
        right = jnp.where(row == j, right_row, right - below * right_row)
    return right


def kernel(
    x_hbm, y_hbm, e_hbm, q_hbm,
    mrg, b_three, r_three, r_own, inverse_out,
    xt, yt, yb, ev, qv,
    tp, tr, tf, qst, qz, qall,
    pp, pr, py, pyr, pa,
    gz, gzr,
    up, ur, uf,
    vp, vr, vs, vyr, vz, vzr, va,
    wp, wr, wy, wyr, wa, rs, ra,
    gp, rnat,
    in_sem, ring_s, ring_r, small_s, small_r,
):
    dp, z = lax.axis_index("dp"), lax.axis_index("shard")
    x, y, c = dp // (2 * NY), (dp // 2) % NY, dp % 2
    m = 2 * x + c

    def device(x_, y_, c_, z_):
        return ((x_ * NY + y_) * 2 + c_, z_)

    z_peers = [device(x, y, c, (z + i) % NZ) for i in range(1, NZ)]
    y_peers = [device(x, (y + i) % NY, c, z) for i in range(1, NY)]
    g_peers = [device(((m + i) % G) // 2, y, (m + i) % 2, z) for i in range(1, G)]

    loads = [
        pltpu.make_async_copy(src, dst, in_sem.at[i])
        for i, (src, dst) in enumerate([(y_hbm, yt), (q_hbm, qv), (x_hbm, xt), (e_hbm, ev)])
    ]
    loads[1].start()
    loads[0].start()
    barrier = pltpu.get_barrier_semaphore()
    for peer in z_peers + y_peers + g_peers:
        pl.semaphore_signal(barrier, inc=1, device_id=peer, device_id_type=MESH)

    def far_first(peers):
        places = range(1, len(peers) + 1)
        return sorted(places, key=lambda i: -min(i, len(peers) + 1 - i))

    stages = {}

    def exchange(stage, peers, src, dst, buffer):
        for i in far_first(peers):
            pltpu.make_async_remote_copy(
                src_ref=src(i), dst_ref=dst(i), send_sem=small_s.at[stage], recv_sem=small_r.at[stage],
                device_id=peers[i - 1], device_id_type=MESH,
            ).start()
        stages[stage] = buffer.at[pl.ds(1, len(peers))]
        return stage

    def arrived(stage):
        pltpu.make_async_copy(stages[stage], stages[stage], small_r.at[stage]).wait()

    def all_sent():
        for stage, pieces in stages.items():
            pltpu.make_async_copy(pieces, pieces, small_s.at[stage]).wait()
        pieces = yb.at[pl.ds(0, NZ - 1)]
        pltpu.make_async_copy(pieces, pieces, ring_s.at[0]).wait()

    def in_order(parts, place, count):
        total = parts[place]
        for owner in range(1, count):
            total = total + parts[(place + count - owner) % count]
        return total

    def cut(a, tile):
        for i in range(G):
            r, l = i % 4, i // 4
            width = min(128, OWN - 128 * l)
            piece = a[8 * r : 8 * r + 8, 128 * l : 128 * l + width]
            tile(i)[...] = piece if width == 128 else jnp.pad(piece, ((0, 0), (0, 128 - width)))

    def uncut(tiles, out):
        for k in range(NZ):
            for i in range(G):
                r, l = i % 4, i // 4
                width = min(128, OWN - 128 * l)
                start = OWN * k + 128 * l
                out[8 * r : 8 * r + 8, start : start + width] = tiles[i, k, :, :width]

    def spread(a, parts):
        for k in range(NZ):
            r, l = k % 4, k // 4
            parts[k] = a[8 * r : 8 * r + 8, 384 * l : 384 * l + 384]

    def gathered(parts):
        return jnp.concatenate([jnp.concatenate([parts[r], parts[r + 4]], axis=1) for r in range(4)], axis=0)

    def summed(own, parts, count):
        total = own
        for i in range(1, count):
            total = total + parts[i]
        return total

    sends = [
        [(h, s) for h in range(NZ // 2) for s in range(SUBS) if h < NZ // 2 - 1 or (s < SUBS // 2) == (d == 0)]
        for d in range(2)
    ]
    ring = {}
    received = set()
    neighbours = (device(x, y, c, (z + 1) % NZ), device(x, y, c, (z + NZ - 1) % NZ))

    def ring_copy(d, h, s):
        owner = (z + NZ - h) % NZ if d == 0 else (z + h) % NZ
        part = yb.at[owner, pl.ds(s * SUB, SUB)]
        return pltpu.make_async_remote_copy(
            src_ref=part, dst_ref=part, send_sem=ring_s.at[0], recv_sem=ring_r.at[d, h, s],
            device_id=neighbours[d], device_id_type=MESH,
        )

    def landed(d, h, s):
        if (d, h, s) not in received:
            received.add((d, h, s))
            ring[d, h, s].wait_recv()

    done = [0]

    def ticks(count):
        for _ in range(count):
            n = done[0]
            if n >= len(sends[0]):
                return
            for d in range(2):
                h, s = sends[d][n]
                if h > 0:
                    landed(d, h - 1, s)
                ring[d, h, s] = ring_copy(d, h, s)
                ring[d, h, s].start()
            done[0] += 1

    loads[1].wait()
    q_own = qv[...]
    cut(q_own, lambda i: qst.at[i])
    qz[z] = qst[m]
    pl.semaphore_wait(barrier, (NZ - 1) + (NY - 1) + (G - 1))
    q_tiles = exchange(0, z_peers, lambda i: qst.at[m], lambda i: qz.at[z], qz)
    loads[0].wait()
    loads[2].start()
    loads[3].start()
    spread(folded(nn(halves(q_own), yt[...])), tp)
    t_sums = exchange(1, z_peers, lambda i: tp.at[(z + i) % NZ], lambda i: tr.at[i], tr)
    yb[z] = yt[...].T
    ticks(1)
    arrived(q_tiles)
    qall[m] = qz[...]
    q_blocks = exchange(2, g_peers, lambda i: qz, lambda i: qall.at[m], qall)
    arrived(t_sums)
    tf[z] = summed(tp[z], tr, NZ)
    t_parts = exchange(3, z_peers, lambda i: tf.at[z], lambda i: tf.at[z], tf)
    ticks(2)
    pp[...] = jnp.zeros(pp.shape, F32)
    loads[2].wait()
    loads[3].wait()
    arrived(q_blocks)
    uncut(qall, rnat)
    p_error = folded(nt(halves(rnat[...]), ev[...]))
    arrived(t_parts)
    p_own = folded(nt(halves(gathered(tf)), xt[...])) + p_error
    for i in range(G):
        x_, c_ = i // 2, i % 2
        width = min(128, ROWS - 128 * x_)
        pp[i, :, :width] = p_own[16 * c_ : 16 * c_ + 16, 128 * x_ : 128 * x_ + width]

    p_sums = exchange(4, g_peers, lambda i: pp.at[(m + i) % G], lambda i: pr.at[i], pr)
    ticks(2)
    arrived(p_sums)
    py[...] = summed(pp[m], pr, G)
    p_rows = exchange(5, y_peers, lambda i: py, lambda i: pyr.at[i], pyr)
    ticks(2)
    arrived(p_rows)
    pyr[0] = py[...]
    pa[m] = in_order(pyr, y, NY)
    p_parts = exchange(6, g_peers, lambda i: pa.at[m], lambda i: pa.at[m], pa)
    ticks(2)
    arrived(p_parts)
    p_all = jnp.concatenate(
        [jnp.concatenate([pa[2 * x_ + c_] for x_ in range(NX)], axis=1) for c_ in range(2)], axis=0
    )[:, :ROWS]

    def gradients(first, count):
        def one(i, carry):
            owner = (z + first + i) % NZ
            gp[owner] = nn(xt[...], yb[owner])
            return carry

        lax.fori_loop(0, count, one, 0)

    def landed_steps(steps):
        for d in range(2):
            for h, s in sends[d]:
                if h in steps:
                    landed(d, h, s)

    p_halves = halves(p_all)
    spread(folded(nn(p_halves, xt[...])), up)
    u_sums = exchange(7, z_peers, lambda i: up.at[(z + i) % NZ], lambda i: ur.at[i], ur)
    v_own = folded(nn(p_halves, ev[...]))
    for k in range(NZ):
        cut(v_own[:, OWN * k : OWN * k + OWN], lambda i: vp.at[i, k])
    v_sums = exchange(8, g_peers, lambda i: vp.at[(m + i) % G], lambda i: vr.at[i], vr)
    ticks(2)
    arrived(u_sums)
    uf[z] = summed(up[z], ur, NZ)
    u_parts = exchange(9, z_peers, lambda i: uf.at[z], lambda i: uf.at[z], uf)
    gram = lax.dot_general(p_all, p_all, (((1,), (1,)), ((), ())), precision=HIGHEST, preferred_element_type=F32)
    for r in range(4):
        gz[:, 32 * r : 32 * r + 32] = gram[8 * r : 8 * r + 8]
    grams = exchange(10, z_peers, lambda i: gz, lambda i: gzr.at[i], gzr)
    arrived(v_sums)
    vs[...] = summed(vp[m], vr, G)
    v_rows = exchange(11, y_peers, lambda i: vs.at[(y + i) % NY], lambda i: vyr.at[i], vyr)
    ticks(2)
    arrived(u_parts)
    w_own = folded(nn(halves(gathered(uf)), yb[z]))
    cut(w_own, lambda i: wp.at[i])
    w_sums = exchange(12, g_peers, lambda i: wp.at[(m + i) % G], lambda i: wr.at[i], wr)
    arrived(v_rows)
    vz[...] = summed(vs[y], vyr, NY)
    v_tiles = exchange(13, z_peers, lambda i: vz, lambda i: vzr.at[i], vzr)
    ticks(100)
    arrived(grams)
    gzr[0] = gz[...]
    total = in_order(gzr, z, NZ)
    gram = jnp.concatenate([total[:, 32 * r : 32 * r + 32] for r in range(4)], axis=0)
    inverse = inverse_factor(gram)
    arrived(w_sums)
    wy[...] = summed(wp[m], wr, G)
    w_rows = exchange(14, y_peers, lambda i: wy, lambda i: wyr.at[i], wyr)
    landed_steps((0, 1))
    gradients(6, 5)
    arrived(w_rows)
    wyr[0] = wy[...]
    wa[z] = in_order(wyr, y, NY)
    w_tiles = exchange(15, z_peers, lambda i: wa.at[z], lambda i: wa.at[z], wa)
    arrived(v_tiles)
    vzr[0] = vz[...]
    va[y] = in_order(vzr, z, NZ)
    v_back = exchange(16, y_peers, lambda i: va.at[y], lambda i: va.at[y], va)
    landed_steps((2, 3))

    def merge(i, carry):
        rows = pl.ds(pl.multiple_of(16 * i, 16), 16)
        for k in range(NZ):
            span = slice(OWN * k, OWN * k + OWN)
            mrg[rows, span] = gp[k, rows, :]
        mrg[rows, :] = mrg[rows, :] + ev[rows, :].astype(F32)
        return carry

    gradients(3, 3)
    p_hat = product(inverse, p_all)
    b = product(inverse.T, p_hat) * (1.0 / WORKERS)
    b_high = b.astype(BF16)
    b_low = (b - b_high.astype(F32)).astype(BF16)
    b_three[...] = jnp.concatenate([b_high, b_high, b_low], axis=0).T
    inverse_out[...] = inverse
    arrived(w_tiles)
    arrived(v_back)
    rs[...] = wa[...] + va[...]
    ra[m] = rs[...]
    r_all = exchange(17, g_peers, lambda i: rs, lambda i: ra.at[m], ra)
    lax.fori_loop(0, ROWS // 16, merge, 0)
    arrived(r_all)
    uncut(ra, rnat)
    r_all = rnat[...]
    r_high = r_all.astype(BF16)
    r_low = (r_all - r_high.astype(F32)).astype(BF16)
    r_three[...] = jnp.concatenate([r_high, r_low, r_high], axis=0)
    r_own[...] = jnp.concatenate([jnp.concatenate([ra[r, z], ra[r + 4, z]], axis=1) for r in range(4)], axis=0)
    all_sent()


def finish(mrg, b_three, r_three, r_own, inverse, out_hbm, q_out, outv, q_own, out_sem):
    stores = []
    for i, (first, count) in enumerate([(0, 128), (128, 128), (256, 128), (384, 112)]):
        rows = slice(first, first + count)
        outv[rows, :] = (mrg[rows, :] - nn(b_three[rows, :], r_three[...])).astype(BF16)
        store = pltpu.make_async_copy(outv.at[pl.ds(first, count)], out_hbm.at[pl.ds(first, count)], out_sem.at[i])
        store.start()
        stores.append(store)
    q_own[...] = (product(inverse[...], r_own[...]) * (1.0 / WORKERS))[:, :OWN]
    stores.append(pltpu.make_async_copy(q_own, q_out, out_sem.at[4]))
    stores[-1].start()
    for store in stores:
        store.wait()


def on_device(layer_input, output_grad, error_buffer, q_start):
    hbm, vmem = pl.BlockSpec(memory_space=pltpu.HBM), pl.BlockSpec(memory_space=pltpu.VMEM)
    merged, b_three, r_three, r_own, inverse = pl.pallas_call(
        kernel,
        out_shape=(
            jax.ShapeDtypeStruct((ROWS, COLS), F32), jax.ShapeDtypeStruct((ROWS, 3 * RANK), BF16),
            jax.ShapeDtypeStruct((3 * RANK, COLS), BF16), jax.ShapeDtypeStruct((RANK, 256), F32),
            jax.ShapeDtypeStruct((RANK, RANK), F32),
        ),
        in_specs=[hbm] * 4,
        out_specs=(vmem,) * 5,
        scratch_shapes=[
            pltpu.VMEM((ROWS, TOK), BF16), pltpu.VMEM((OWN, TOK), BF16), pltpu.VMEM((NZ, TOK, OWN), BF16),
            pltpu.VMEM((ROWS, COLS), BF16), pltpu.VMEM((RANK, OWN), F32),
            pltpu.VMEM((NZ, 8, 384), F32), pltpu.VMEM((NZ, 8, 384), F32), pltpu.VMEM((NZ, 8, 384), F32),
            pltpu.VMEM((G, 8, 128), F32), pltpu.VMEM((NZ, 8, 128), F32), pltpu.VMEM((G, NZ, 8, 128), F32),
            pltpu.VMEM((G, 16, 128), F32), pltpu.VMEM((G, 16, 128), F32), pltpu.VMEM((16, 128), F32),
            pltpu.VMEM((NY, 16, 128), F32), pltpu.VMEM((G, 16, 128), F32),
            pltpu.VMEM((8, 128), F32), pltpu.VMEM((NZ, 8, 128), F32),
            pltpu.VMEM((NZ, 8, 384), F32), pltpu.VMEM((NZ, 8, 384), F32), pltpu.VMEM((NZ, 8, 384), F32),
            pltpu.VMEM((G, NZ, 8, 128), F32), pltpu.VMEM((G, NZ, 8, 128), F32), pltpu.VMEM((NZ, 8, 128), F32),
            pltpu.VMEM((NY, 8, 128), F32), pltpu.VMEM((8, 128), F32), pltpu.VMEM((NZ, 8, 128), F32),
            pltpu.VMEM((NY, 8, 128), F32),
            pltpu.VMEM((G, 8, 128), F32), pltpu.VMEM((G, 8, 128), F32), pltpu.VMEM((8, 128), F32),
            pltpu.VMEM((NY, 8, 128), F32), pltpu.VMEM((NZ, 8, 128), F32), pltpu.VMEM((NZ, 8, 128), F32),
            pltpu.VMEM((G, NZ, 8, 128), F32),
            pltpu.VMEM((NZ, ROWS, OWN), F32), pltpu.VMEM((RANK, COLS), F32),
            pltpu.SemaphoreType.DMA((4,)),
            pltpu.SemaphoreType.DMA((1,)), pltpu.SemaphoreType.DMA((2, NZ // 2, SUBS)),
            pltpu.SemaphoreType.DMA((18,)), pltpu.SemaphoreType.DMA((18,)),
        ],
        compiler_params=pltpu.CompilerParams(
            collective_id=0, has_side_effects=True, vmem_limit_bytes=40 * 2**20
        ),
    )(*(
        pltpu.with_memory_space_constraint(a, pltpu.HBM)
        for a in (layer_input.T, output_grad.T, error_buffer[0], q_start.T)
    ))
    new_error, q_factor = pl.pallas_call(
        finish,
        out_shape=(jax.ShapeDtypeStruct((ROWS, COLS), BF16), jax.ShapeDtypeStruct((RANK, OWN), F32)),
        in_specs=[vmem] * 5,
        out_specs=(hbm, hbm),
        scratch_shapes=[pltpu.VMEM((ROWS, COLS), BF16), pltpu.VMEM((RANK, OWN), F32), pltpu.SemaphoreType.DMA((5,))],
        compiler_params=pltpu.CompilerParams(vmem_limit_bytes=16 * 2**20),
    )(merged, b_three, r_three, r_own, inverse)
    return (new_error[None], q_factor.T)


def solution(mesh):
    return jax.shard_map(
        on_device,
        mesh=mesh,
        in_specs=(P("dp", "shard"), P("dp", "shard"), P("dp", "shard", None), P("shard", None)),
        out_specs=(P("dp", "shard", None), P("shard", None)),
        check_vma=False,
    )
```

```python
import functools

import jax
import jax.numpy as jnp
from jax import lax
from jax.experimental import pallas as pl
from jax.experimental.pallas import tpu as pltpu
from jax.sharding import PartitionSpec as P

MESH = pl.DeviceIdType.MESH
F32, BF16 = jnp.float32, jnp.bfloat16
NX, NY, NZ = 4, 8, 8
G = 2 * NX
TOK, ROWS, COLS, OWN, RANK = 768, 496, 1984, 248, 32
SUBS = 2
SUB = TOK // SUBS
WORKERS = 64
HIGHEST = lax.Precision.HIGHEST


def halves(a):
    high = a.astype(BF16)
    low = (a - high.astype(F32)).astype(BF16)
    return jnp.concatenate([high, low], axis=0)


def folded(a):
    return a[:RANK] + a[RANK:]


def nn(a, b):
    return lax.dot_general(a, b, (((1,), (0,)), ((), ())), preferred_element_type=F32)


def nt(a, b):
    return lax.dot_general(a, b, (((1,), (1,)), ((), ())), preferred_element_type=F32)


def thirds(a):
    high = a.astype(BF16)
    rest = a - high.astype(F32)
    middle = rest.astype(BF16)
    return high, middle, (rest - middle.astype(F32)).astype(BF16)


def product(a, b):
    a0, a1, a2 = thirds(a)
    b0, b1, b2 = thirds(b)
    return nn(jnp.concatenate([a0, a0, a0, a1, a1, a2], axis=1), jnp.concatenate([b0, b1, b2, b0, b1, b0], axis=0))


def inverse_factor(gram):
    row = lax.broadcasted_iota(jnp.int32, (RANK, RANK), 0)
    col = lax.broadcasted_iota(jnp.int32, (RANK, RANK), 1)
    left, right = gram, jnp.where(row == col, 1.0, 0.0).astype(F32)
    index = lax.broadcasted_iota(jnp.int32, (RANK, 1), 0)
    for j in range(RANK):
        scale = 1.0 / jnp.sqrt(left[j : j + 1, j : j + 1])
        left_row, right_row = left[j : j + 1, :] * scale, right[j : j + 1, :] * scale
        column = left[:, j : j + 1] * scale
        below = jnp.where(index > j, column, 0.0)
        left = left - below * left_row
        right = jnp.where(row == j, right_row, right - below * right_row)
    return right


def kernel(
    x_hbm, y_hbm, e_hbm, q_hbm,
    mrg, b_three, r_three, r_own, inverse_out,
    xt, yt, yb, ev, qv,
    tp, tr, tf, qst, qz, qall,
    pp, pr, py, pyr, pa,
    gz, gzr,
    up, ur, uf,
    vp, vr, vs, vyr, vz, vzr, va,
    wp, wr, wy, wyr, wa, rs, ra,
    gp, rnat,
    in_sem, ring_s, ring_r, small_s, small_r,
):
    dp, z = lax.axis_index("dp"), lax.axis_index("shard")
    x, y, c = dp // (2 * NY), (dp // 2) % NY, dp % 2
    m = 2 * x + c

    def device(x_, y_, c_, z_):
        return ((x_ * NY + y_) * 2 + c_, z_)

    z_peers = [device(x, y, c, (z + i) % NZ) for i in range(1, NZ)]
    y_peers = [device(x, (y + i) % NY, c, z) for i in range(1, NY)]
    g_peers = [device(((m + i) % G) // 2, y, (m + i) % 2, z) for i in range(1, G)]

    loads = [
        pltpu.make_async_copy(src, dst, in_sem.at[i])
        for i, (src, dst) in enumerate([(y_hbm, yt), (q_hbm, qv), (x_hbm, xt), (e_hbm, ev)])
    ]
    for load in loads:
        load.start()
    barrier = pltpu.get_barrier_semaphore()
    for peer in z_peers + y_peers + g_peers:
        pl.semaphore_signal(barrier, inc=1, device_id=peer, device_id_type=MESH)

    def far_first(peers):
        places = range(1, len(peers) + 1)
        return sorted(places, key=lambda i: -min(i, len(peers) + 1 - i))

    stages = {}

    def exchange(stage, peers, src, dst, buffer):
        for i in far_first(peers):
            pltpu.make_async_remote_copy(
                src_ref=src(i), dst_ref=dst(i), send_sem=small_s.at[stage], recv_sem=small_r.at[stage],
                device_id=peers[i - 1], device_id_type=MESH,
            ).start()
        stages[stage] = buffer.at[pl.ds(1, len(peers))]
        return stage

    def arrived(stage):
        pltpu.make_async_copy(stages[stage], stages[stage], small_r.at[stage]).wait()

    def all_sent():
        for stage, pieces in stages.items():
            pltpu.make_async_copy(pieces, pieces, small_s.at[stage]).wait()
        pieces = yb.at[pl.ds(0, NZ - 1)]
        pltpu.make_async_copy(pieces, pieces, ring_s.at[0]).wait()

    def in_order(parts, place, count):
        total = parts[place]
        for owner in range(1, count):
            total = total + parts[(place + count - owner) % count]
        return total

    def cut(a, tile):
        for i in range(G):
            r, l = i % 4, i // 4
            width = min(128, OWN - 128 * l)
            piece = a[8 * r : 8 * r + 8, 128 * l : 128 * l + width]
            tile(i)[...] = piece if width == 128 else jnp.pad(piece, ((0, 0), (0, 128 - width)))

    def uncut(tiles, out):
        for k in range(NZ):
            for i in range(G):
                r, l = i % 4, i // 4
                width = min(128, OWN - 128 * l)
                start = OWN * k + 128 * l
                out[8 * r : 8 * r + 8, start : start + width] = tiles[i, k, :, :width]

    def spread(a, parts):
        for k in range(NZ):
            r, l = k % 4, k // 4
            parts[k] = a[8 * r : 8 * r + 8, 384 * l : 384 * l + 384]

    def gathered(parts):
        return jnp.concatenate([jnp.concatenate([parts[r], parts[r + 4]], axis=1) for r in range(4)], axis=0)

    def summed(own, parts, count):
        total = own
        for i in range(1, count):
            total = total + parts[i]
        return total

    sends = [
        [(h, s) for h in range(NZ // 2) for s in range(SUBS) if h < NZ // 2 - 1 or (s < SUBS // 2) == (d == 0)]
        for d in range(2)
    ]
    ring = {}
    received = set()
    neighbours = (device(x, y, c, (z + 1) % NZ), device(x, y, c, (z + NZ - 1) % NZ))

    def ring_copy(d, h, s):
        owner = (z + NZ - h) % NZ if d == 0 else (z + h) % NZ
        part = yb.at[owner, pl.ds(s * SUB, SUB)]
        return pltpu.make_async_remote_copy(
            src_ref=part, dst_ref=part, send_sem=ring_s.at[0], recv_sem=ring_r.at[d, h, s],
            device_id=neighbours[d], device_id_type=MESH,
        )

    def landed(d, h, s):
        if (d, h, s) not in received:
            received.add((d, h, s))
            ring[d, h, s].wait_recv()

    done = [0]

    def ticks(count):
        for _ in range(count):
            n = done[0]
            if n >= len(sends[0]):
                return
            for d in range(2):
                h, s = sends[d][n]
                if h > 0:
                    landed(d, h - 1, s)
                ring[d, h, s] = ring_copy(d, h, s)
                ring[d, h, s].start()
            done[0] += 1

    loads[0].wait()
    loads[1].wait()
    q_own = qv[...]
    cut(q_own, lambda i: qst.at[i])
    qz[z] = qst[m]
    t_own = folded(nn(halves(q_own), yt[...]))
    spread(t_own, tp)
    pl.semaphore_wait(barrier, (NZ - 1) + (NY - 1) + (G - 1))

    q_tiles = exchange(0, z_peers, lambda i: qst.at[m], lambda i: qz.at[z], qz)
    t_sums = exchange(1, z_peers, lambda i: tp.at[(z + i) % NZ], lambda i: tr.at[i], tr)
    yb[z] = yt[...].T
    ticks(1)
    arrived(q_tiles)
    qall[m] = qz[...]
    q_blocks = exchange(2, g_peers, lambda i: qz, lambda i: qall.at[m], qall)
    arrived(t_sums)
    tf[z] = summed(tp[z], tr, NZ)
    t_parts = exchange(3, z_peers, lambda i: tf.at[z], lambda i: tf.at[z], tf)
    ticks(1)
    pp[...] = jnp.zeros(pp.shape, F32)
    loads[2].wait()
    loads[3].wait()
    arrived(q_blocks)
    uncut(qall, rnat)
    p_error = folded(nt(halves(rnat[...]), ev[...]))
    arrived(t_parts)
    p_own = folded(nt(halves(gathered(tf)), xt[...])) + p_error
    for i in range(G):
        x_, c_ = i // 2, i % 2
        width = min(128, ROWS - 128 * x_)
        pp[i, :, :width] = p_own[16 * c_ : 16 * c_ + 16, 128 * x_ : 128 * x_ + width]

    p_sums = exchange(4, g_peers, lambda i: pp.at[(m + i) % G], lambda i: pr.at[i], pr)
    ticks(1)
    arrived(p_sums)
    py[...] = summed(pp[m], pr, G)
    p_rows = exchange(5, y_peers, lambda i: py, lambda i: pyr.at[i], pyr)
    ticks(1)
    arrived(p_rows)
    pyr[0] = py[...]
    pa[m] = in_order(pyr, y, NY)
    p_parts = exchange(6, g_peers, lambda i: pa.at[m], lambda i: pa.at[m], pa)
    ticks(1)
    arrived(p_parts)
    p_all = jnp.concatenate(
        [jnp.concatenate([pa[2 * x_ + c_] for x_ in range(NX)], axis=1) for c_ in range(2)], axis=0
    )[:, :ROWS]

    def gradients(first, count):
        def one(i, carry):
            owner = (z + first + i) % NZ
            gp[owner] = nn(xt[...], yb[owner])
            return carry

        lax.fori_loop(0, count, one, 0)

    def landed_steps(steps):
        for d in range(2):
            for h, s in sends[d]:
                if h in steps:
                    landed(d, h, s)

    p_halves = halves(p_all)
    spread(folded(nn(p_halves, xt[...])), up)
    u_sums = exchange(7, z_peers, lambda i: up.at[(z + i) % NZ], lambda i: ur.at[i], ur)
    v_own = folded(nn(p_halves, ev[...]))
    for k in range(NZ):
        cut(v_own[:, OWN * k : OWN * k + OWN], lambda i: vp.at[i, k])
    v_sums = exchange(8, g_peers, lambda i: vp.at[(m + i) % G], lambda i: vr.at[i], vr)
    ticks(1)
    arrived(u_sums)
    uf[z] = summed(up[z], ur, NZ)
    u_parts = exchange(9, z_peers, lambda i: uf.at[z], lambda i: uf.at[z], uf)
    gram = lax.dot_general(p_all, p_all, (((1,), (1,)), ((), ())), precision=HIGHEST, preferred_element_type=F32)
    for r in range(4):
        gz[:, 32 * r : 32 * r + 32] = gram[8 * r : 8 * r + 8]
    grams = exchange(10, z_peers, lambda i: gz, lambda i: gzr.at[i], gzr)
    arrived(v_sums)
    vs[...] = summed(vp[m], vr, G)
    v_rows = exchange(11, y_peers, lambda i: vs.at[(y + i) % NY], lambda i: vyr.at[i], vyr)
    ticks(1)
    arrived(u_parts)
    w_own = folded(nn(halves(gathered(uf)), yb[z]))
    cut(w_own, lambda i: wp.at[i])
    w_sums = exchange(12, g_peers, lambda i: wp.at[(m + i) % G], lambda i: wr.at[i], wr)
    arrived(v_rows)
    vz[...] = summed(vs[y], vyr, NY)
    v_tiles = exchange(13, z_peers, lambda i: vz, lambda i: vzr.at[i], vzr)
    ticks(100)
    arrived(grams)
    gzr[0] = gz[...]
    total = in_order(gzr, z, NZ)
    gram = jnp.concatenate([total[:, 32 * r : 32 * r + 32] for r in range(4)], axis=0)
    inverse = inverse_factor(gram)
    arrived(w_sums)
    wy[...] = summed(wp[m], wr, G)
    w_rows = exchange(14, y_peers, lambda i: wy, lambda i: wyr.at[i], wyr)
    landed_steps((0, 1))
    gradients(6, 5)
    arrived(w_rows)
    wyr[0] = wy[...]
    wa[z] = in_order(wyr, y, NY)
    w_tiles = exchange(15, z_peers, lambda i: wa.at[z], lambda i: wa.at[z], wa)
    arrived(v_tiles)
    vzr[0] = vz[...]
    va[y] = in_order(vzr, z, NZ)
    v_back = exchange(16, y_peers, lambda i: va.at[y], lambda i: va.at[y], va)
    landed_steps((2, 3))

    def merge(i, carry):
        rows = pl.ds(pl.multiple_of(16 * i, 16), 16)
        for k in range(NZ):
            span = slice(OWN * k, OWN * k + OWN)
            mrg[rows, span] = gp[k, rows, :] + ev[rows, span].astype(F32)
        return carry

    gradients(3, 3)
    arrived(w_tiles)
    arrived(v_back)
    rs[...] = wa[...] + va[...]
    ra[m] = rs[...]
    r_all = exchange(17, g_peers, lambda i: rs, lambda i: ra.at[m], ra)
    lax.fori_loop(0, ROWS // 16, merge, 0)
    p_hat = product(inverse, p_all)
    b = product(inverse.T, p_hat) * (1.0 / WORKERS)
    b_high = b.astype(BF16)
    b_low = (b - b_high.astype(F32)).astype(BF16)
    b_three[...] = jnp.concatenate([b_high, b_high, b_low], axis=0).T
    inverse_out[...] = inverse
    arrived(r_all)
    uncut(ra, rnat)
    r_all = rnat[...]
    r_high = r_all.astype(BF16)
    r_low = (r_all - r_high.astype(F32)).astype(BF16)
    r_three[...] = jnp.concatenate([r_high, r_low, r_high], axis=0)
    r_own[...] = jnp.concatenate([jnp.concatenate([ra[r, z], ra[r + 4, z]], axis=1) for r in range(4)], axis=0)
    all_sent()


def finish(mrg, b_three, r_three, r_own, inverse, out_hbm, q_out, outv, q_own, out_sem):
    stores = []
    for i, (first, count) in enumerate([(0, 128), (128, 128), (256, 128), (384, 112)]):
        rows = slice(first, first + count)
        outv[rows, :] = (mrg[rows, :] - nn(b_three[rows, :], r_three[...])).astype(BF16)
        store = pltpu.make_async_copy(outv.at[pl.ds(first, count)], out_hbm.at[pl.ds(first, count)], out_sem.at[i])
        store.start()
        stores.append(store)
    q_own[...] = (product(inverse[...], r_own[...]) * (1.0 / WORKERS))[:, :OWN]
    stores.append(pltpu.make_async_copy(q_own, q_out, out_sem.at[4]))
    stores[-1].start()
    for store in stores:
        store.wait()


def on_device(layer_input, output_grad, error_buffer, q_start):
    hbm, vmem = pl.BlockSpec(memory_space=pltpu.HBM), pl.BlockSpec(memory_space=pltpu.VMEM)
    merged, b_three, r_three, r_own, inverse = pl.pallas_call(
        kernel,
        out_shape=(
            jax.ShapeDtypeStruct((ROWS, COLS), F32), jax.ShapeDtypeStruct((ROWS, 3 * RANK), BF16),
            jax.ShapeDtypeStruct((3 * RANK, COLS), BF16), jax.ShapeDtypeStruct((RANK, 256), F32),
            jax.ShapeDtypeStruct((RANK, RANK), F32),
        ),
        in_specs=[hbm] * 4,
        out_specs=(vmem,) * 5,
        scratch_shapes=[
            pltpu.VMEM((ROWS, TOK), BF16), pltpu.VMEM((OWN, TOK), BF16), pltpu.VMEM((NZ, TOK, OWN), BF16),
            pltpu.VMEM((ROWS, COLS), BF16), pltpu.VMEM((RANK, OWN), F32),
            pltpu.VMEM((NZ, 8, 384), F32), pltpu.VMEM((NZ, 8, 384), F32), pltpu.VMEM((NZ, 8, 384), F32),
            pltpu.VMEM((G, 8, 128), F32), pltpu.VMEM((NZ, 8, 128), F32), pltpu.VMEM((G, NZ, 8, 128), F32),
            pltpu.VMEM((G, 16, 128), F32), pltpu.VMEM((G, 16, 128), F32), pltpu.VMEM((16, 128), F32),
            pltpu.VMEM((NY, 16, 128), F32), pltpu.VMEM((G, 16, 128), F32),
            pltpu.VMEM((8, 128), F32), pltpu.VMEM((NZ, 8, 128), F32),
            pltpu.VMEM((NZ, 8, 384), F32), pltpu.VMEM((NZ, 8, 384), F32), pltpu.VMEM((NZ, 8, 384), F32),
            pltpu.VMEM((G, NZ, 8, 128), F32), pltpu.VMEM((G, NZ, 8, 128), F32), pltpu.VMEM((NZ, 8, 128), F32),
            pltpu.VMEM((NY, 8, 128), F32), pltpu.VMEM((8, 128), F32), pltpu.VMEM((NZ, 8, 128), F32),
            pltpu.VMEM((NY, 8, 128), F32),
            pltpu.VMEM((G, 8, 128), F32), pltpu.VMEM((G, 8, 128), F32), pltpu.VMEM((8, 128), F32),
            pltpu.VMEM((NY, 8, 128), F32), pltpu.VMEM((NZ, 8, 128), F32), pltpu.VMEM((NZ, 8, 128), F32),
            pltpu.VMEM((G, NZ, 8, 128), F32),
            pltpu.VMEM((NZ, ROWS, OWN), F32), pltpu.VMEM((RANK, COLS), F32),
            pltpu.SemaphoreType.DMA((4,)),
            pltpu.SemaphoreType.DMA((1,)), pltpu.SemaphoreType.DMA((2, NZ // 2, SUBS)),
            pltpu.SemaphoreType.DMA((18,)), pltpu.SemaphoreType.DMA((18,)),
        ],
        compiler_params=pltpu.CompilerParams(
            collective_id=0, has_side_effects=True, vmem_limit_bytes=40 * 2**20
        ),
    )(*(
        pltpu.with_memory_space_constraint(a, pltpu.HBM)
        for a in (layer_input.T, output_grad.T, error_buffer[0], q_start.T)
    ))
    new_error, q_factor = pl.pallas_call(
        finish,
        out_shape=(jax.ShapeDtypeStruct((ROWS, COLS), BF16), jax.ShapeDtypeStruct((RANK, OWN), F32)),
        in_specs=[vmem] * 5,
        out_specs=(hbm, hbm),
        scratch_shapes=[pltpu.VMEM((ROWS, COLS), BF16), pltpu.VMEM((RANK, OWN), F32), pltpu.SemaphoreType.DMA((5,))],
        compiler_params=pltpu.CompilerParams(vmem_limit_bytes=16 * 2**20),
    )(merged, b_three, r_three, r_own, inverse)
    return (new_error[None], q_factor.T)


def solution(mesh):
    return jax.shard_map(
        on_device,
        mesh=mesh,
        in_specs=(P("dp", "shard"), P("dp", "shard"), P("dp", "shard", None), P("shard", None)),
        out_specs=(P("dp", "shard", None), P("shard", None)),
        check_vma=False,
    )
```
